32 devices in a mesh: lev: 4 (over x, core), lon: 8 (over z, y).
Axes of the slice: x: 2, y: 2, z: 4, core: 2. Of those that a mesh axis runs over, the one named last changes fastest.
Arguments:
- wave_state: float32 [3, 128, 8, 2048], P(None, 'lev', None, 'lon'), may hold values from -6 to 6
- to_modes: float32 [128, 128], replicated, may hold values from -1 to 2.5
- from_modes: float32 [128, 128], replicated, may hold values from -1 to 2.5
- courant: float32 [128], P('lev'), may hold values from 0.25 to 4
- shifts: float32 [3], replicated, may hold values from 0.5 to 2
Outputs:
- advanced: float32 [3, 128, 8, 2048], P(None, 'lev', None, 'lon')
The draws below stay inside these ranges and needn't reach their ends.
All inputs are finite; a program needn't handle non-finite values.
Results may differ from the reference program's by a relative error of at most 0.004.
Values sent between devices are 32-bit elements; how exact they have to be, the bound alone decides.
A program may use at most 64 MiB of HBM per device.

```python
import math
import jax
import jax.numpy as jnp
from jax import lax

LEV = 128
LAT = 8
KDIM = 4
SWEEPS = 3
SQUARINGS = 16
TAYLOR = 8
SHIFTS = 3
NLON = 2048
N_LEV = 4


def square_matrix(key, salt):
    inner_key = jax.random.fold_in(key, salt)
    key_diag, key_off = jax.random.split(inner_key)
    identity = jnp.eye(LEV, dtype=jnp.float32)
    diagonal = jax.random.uniform(key_diag, (LEV,), jnp.float32, 1.0, 2.0)
    spread = jnp.clip(jax.random.normal(key_off, (LEV, LEV), jnp.float32), -4.0, 4.0) * (0.2 / math.sqrt(LEV))
    return spread * (1.0 - identity) + diagonal[:, None] * identity


def draw_to_modes(key, part):
    return square_matrix(key, 11)


def draw_from_modes(key, part):
    return square_matrix(key, 23)


def block_scale(rng, extent, cuts, low, top_value):
    level = 1.0
    for dim, parts in cuts:
        steps = jax.random.uniform(jax.random.fold_in(jax.random.fold_in(rng, 6), dim), (parts,), jnp.float32, low / len(cuts), top_value / len(cuts))
        level = level * jnp.repeat(jnp.exp(steps), extent[dim] // parts).reshape((-1,) + (1,) * (len(extent) - 1 - dim))
    return level


def gaussian(stream_key, shape, deviation, bound, cuts=(), kind=jnp.bfloat16):
    gain = block_scale(stream_key, shape, cuts, -0.22, 0.18) if cuts else 1.0
    values = jax.random.normal(stream_key, shape, jnp.float32) * deviation * gain
    return jnp.minimum(jnp.maximum(values, -bound), bound).astype(kind)


def setup_inputs(seed: int = 0) -> dict:
    streams_of = jax.random.split(jax.random.key(seed), 6)
    wave_state = gaussian(streams_of[0], (3, LEV, LAT, NLON), 1.0, 6.0, ((1, 4), (3, 8)), jnp.float32)
    to_modes = draw_to_modes(jax.random.fold_in(streams_of[5], 71), 0)
    from_modes = draw_from_modes(jax.random.fold_in(streams_of[5], 71), 0)
    courant = jnp.clip(jnp.exp(math.log(4.0) - 2.7725887 * jax.random.uniform(streams_of[3], (LEV,), jnp.float32) ** block_scale(streams_of[3], (LEV,), ((0, 4),), -0.2, 0.2)), 0.25, 4.0)
    shifts = jnp.clip(jnp.exp(jax.random.uniform(streams_of[4], (SHIFTS,), jnp.float32, math.log(0.5), math.log(2.0))), 0.5, 2.0)
    return {"wave_state": wave_state, "to_modes": to_modes, "from_modes": from_modes, "courant": courant, "shifts": shifts}


highest = lax.Precision.HIGHEST
epsilon = 1e-06

def geometry(lon_cells, rows):
    spacing = 2.0 * math.pi / lon_cells
    row_index = jnp.arange(rows, dtype=jnp.float32)
    centre = jnp.sin((row_index + 0.5) * spacing)
    face_sin = jnp.where(row_index < rows - 1, jnp.sin((row_index + 1.0) * spacing), 0.0)
    face_below = jnp.concatenate([jnp.zeros((1,), jnp.float32), face_sin[:-1]])
    return (centre[:, None], face_sin[:, None], face_below[:, None])

def geometric_run(values, decay_rate, reverse):
    length = values.shape[-1]
    result = values
    stride = 1
    while stride < length:
        factor = jnp.exp(-decay_rate * stride)
        if reverse:
            shifted = jnp.concatenate([result[..., stride:], jnp.zeros_like(result[..., :stride])], axis=-1)
        else:
            shifted = jnp.concatenate([jnp.zeros_like(result[..., :stride]), result[..., :-stride]], axis=-1)
        result = result + factor * shifted
        stride = stride * 2
    return result

def line_terms(courant, shift_value, geometry_terms):
    centre, face_sin, face_below = geometry_terms
    wave_speed = courant[:, None, None]
    zonal_coef = wave_speed / (centre * centre)
    merid_diag = wave_speed * (face_sin + face_below) / centre
    half_ratio = 0.5 * (shift_value * shift_value + merid_diag) / zonal_coef
    decay_rate = jnp.log1p(half_ratio + jnp.sqrt(half_ratio * (half_ratio + 2.0)))
    return (zonal_coef, decay_rate)

def line_inverse(right_side, zonal_coef, decay_rate):
    length = right_side.shape[-1]
    position = jnp.arange(length, dtype=jnp.float32)
    denom = -jnp.expm1(-decay_rate * length)
    ahead = geometric_run(right_side, decay_rate, False)
    ahead = ahead + jnp.exp(-decay_rate * (position + 1.0)) * ahead[..., -1:] / denom
    behind = geometric_run(ahead, decay_rate, True)
    behind = behind + jnp.exp(-decay_rate * (length - position)) * behind[..., :1] / denom
    return jnp.exp(-decay_rate) / zonal_coef * behind

def north_diff(values):
    return jnp.concatenate([values[..., 1:, :] - values[..., :-1, :], jnp.zeros_like(values[..., :1, :])], axis=-2)

def divergence(east_wind, west_wind, north_wind, geometry_terms):
    centre, face_sin, face_below = geometry_terms
    flux = face_sin * north_wind
    below = jnp.concatenate([jnp.zeros_like(flux[..., :1, :]), flux[..., :-1, :]], axis=-2)
    return (east_wind - west_wind) / centre + (flux - below) / centre

def coupling(values, geometry_terms):
    centre, face_sin, face_below = geometry_terms
    upper = jnp.concatenate([values[..., 1:, :], jnp.zeros_like(values[..., :1, :])], axis=-2)
    lower = jnp.concatenate([jnp.zeros_like(values[..., :1, :]), values[..., :-1, :]], axis=-2)
    return (face_sin * upper + face_below * lower) / centre

def apply_operator(vector, west_u, east_p, courant, geometry_terms):
    centre = geometry_terms[0]
    wave_speed = courant[:, None, None]
    new_east = -(east_p - vector[2]) / centre
    new_north = -north_diff(vector[2])
    new_height = -wave_speed * divergence(vector[0], west_u, vector[1], geometry_terms)
    return jnp.stack([new_east, new_north, new_height])

def inner_product(first_vec, second_vec, courant, geometry_terms):
    centre, face_sin, face_below = geometry_terms
    weighted = centre * first_vec[0] * second_vec[0] + face_sin * first_vec[1] * second_vec[1]
    weighted = weighted + centre / courant[:, None, None] * first_vec[2] * second_vec[2]
    return lax.optimization_barrier(jnp.sum(weighted, axis=(-2, -1)))

def exponential(matrix):
    dimension = matrix.shape[-1]
    identity = jnp.eye(dimension, dtype=matrix.dtype)
    scaled = matrix / float(2 ** SQUARINGS)
    result = jnp.broadcast_to(identity, matrix.shape)
    for degree in range(TAYLOR, 0, -1):
        result = identity + jnp.einsum('mij,mjk->mik', scaled, result, precision=highest) / degree
    for repeat in range(SQUARINGS):
        result = jnp.einsum('mij,mjk->mik', result, result, precision=highest)
    return result

def shifted_solve(vector, courant, shift_value, geometry_terms):
    wave_speed = courant[:, None, None]
    west_u = jnp.roll(vector[0], 1, axis=-1)
    right_side = shift_value * vector[2] - wave_speed * divergence(vector[0], west_u, vector[1], geometry_terms)
    zonal_coef, decay_rate = line_terms(courant, shift_value, geometry_terms)
    solved = jnp.zeros_like(right_side)
    for sweep_no in range(SWEEPS):
        source = right_side + wave_speed * coupling(solved, geometry_terms)
        solved = line_inverse(source, zonal_coef, decay_rate)
    east_p = jnp.roll(solved, -1, axis=-1)
    new_east = (vector[0] - (east_p - solved) / geometry_terms[0]) / shift_value
    new_north = (vector[1] - north_diff(solved)) / shift_value
    return jnp.stack([new_east, new_north, solved])

def advance_modes(modal_fields, courant, shifts, geometry_terms):
    start_norm = jnp.sqrt(inner_product(modal_fields, modal_fields, courant, geometry_terms) + epsilon)
    krylov_basis = [modal_fields / start_norm[:, None, None]]
    for step_no in range(1, KDIM):
        candidate = shifted_solve(krylov_basis[-1], courant, shifts[step_no - 1], geometry_terms)
        projections = jnp.stack([inner_product(earlier, candidate, courant, geometry_terms) for earlier in krylov_basis])
        for number, earlier in enumerate(krylov_basis):
            candidate = candidate - projections[number][:, None, None] * earlier
        new_norm = jnp.sqrt(inner_product(candidate, candidate, courant, geometry_terms) + epsilon)
        krylov_basis.append(candidate / new_norm[:, None, None])
    images = []
    for column_vec in krylov_basis:
        west_u = jnp.roll(column_vec[0], 1, axis=-1)
        east_p = jnp.roll(column_vec[2], -1, axis=-1)
        images.append(apply_operator(column_vec, west_u, east_p, courant, geometry_terms))
    reduced = jnp.stack([jnp.stack([inner_product(row_vec, image, courant, geometry_terms) for image in images], axis=-1) for row_vec in krylov_basis], axis=-2)
    skew_part = 0.5 * (reduced - jnp.swapaxes(reduced, -1, -2))
    propagator = exponential(skew_part)
    mixing = start_norm[:, None] * propagator[:, :, 0]
    result = mixing[:, 0][:, None, None] * krylov_basis[0]
    for number in range(1, KDIM):
        result = result + mixing[:, number][:, None, None] * krylov_basis[number]
    return result

def reference(wave_state, to_modes, from_modes, courant, shifts):
    geometry_terms = geometry(NLON, LAT)
    block_modes = LEV // N_LEV
    modal_fields = jnp.einsum('ml,flac->fmac', to_modes, wave_state, precision=highest)
    blocks = jnp.moveaxis(modal_fields.reshape(3, N_LEV, block_modes, LAT, NLON), 1, 0)
    speed_blocks = courant.reshape(N_LEV, block_modes)

    def advance_block(bundle):
        return advance_modes(bundle[0], bundle[1], shifts, geometry_terms)
    advanced_blocks = lax.map(advance_block, (blocks, speed_blocks))
    advanced_modal = jnp.moveaxis(advanced_blocks, 0, 1).reshape(3, LEV, LAT, NLON)
    return jnp.einsum('ml,flac->fmac', from_modes, advanced_modal, precision=highest)
```

```python
import functools
import math

import jax
import jax.numpy as jnp
from jax import lax
from jax.experimental import pallas as pl
from jax.experimental.pallas import tpu as pltpu
from jax.sharding import PartitionSpec as P

KDIM = 4
SWEEPS = 3
SQUARINGS = 16
TAYLOR = 8
SOLVES = KDIM - 1
LANES = 128
ROWS = 8
MESH = pl.DeviceIdType.MESH
highest = lax.Precision.HIGHEST
epsilon = 1e-06

TILES = []
for _t in range(SOLVES):
    TILES += [_t + 1, 1, 1]
TILES += [2]
OFFSETS = [sum(TILES[:x]) for x in range(len(TILES))]
LAST = len(TILES) - 1


def kernel(n_lev, n_lon, lon_all, modes, cells, x_ref, tm_ref, fm_ref, k_ref, sh_ref, out_ref,
           g_ref, b_ref, u_ref, v_ref, p_ref, src_ref, fa_ref, fb_ref, sol_ref, wa_ref, wb_ref,
           wt_ref, tt_ref, sbuf, rbuf, lev_send, lev_recv, lon_send, lon_recv):
    chunks = LANES // modes
    n_chip = n_lev // 2
    lev = lax.axis_index("lev")
    lon = lax.axis_index("lon")
    chip, core = lev // 2, lev % 2
    partner = chip * 2 + (1 - core)

    def chip_peer(offset):
        return lax.rem(chip + offset, n_chip) * 2 + core

    barrier = pltpu.get_barrier_semaphore()
    for off in range(1, n_lon):
        pl.semaphore_signal(barrier, inc=1, device_id=(lev, lax.rem(lon + off, n_lon)), device_id_type=MESH)
    for off in range(1, n_chip):
        pl.semaphore_signal(barrier, inc=1, device_id=(chip_peer(off), lon), device_id_type=MESH)
    pl.semaphore_signal(barrier, inc=1, device_id=(partner, lon), device_id_type=MESH)
    pl.semaphore_wait(barrier, n_lon - 1 + n_chip)

    def lev_copy(turn, slot_from, slot_to, field, target, send_no):
        return pltpu.make_async_remote_copy(
            src_ref=g_ref.at[turn, slot_from, field],
            dst_ref=g_ref.at[turn, slot_to, field],
            send_sem=lev_send.at[turn, send_no, field],
            recv_sem=lev_recv.at[turn, slot_to, field],
            device_id=(target, lon),
            device_id_type=MESH,
        )

    def start_field(turn, field):
        for off in range(1, n_chip):
            lev_copy(turn, 0, 2 * off, field, chip_peer(off), off - 1).start()
        lev_copy(turn, 0, 1, field, partner, n_chip - 1).start()

    def relay_field(turn, field):
        for off in range(1, n_chip):
            lev_copy(turn, 2 * off, 2 * off, field, chip_peer(off), off - 1).wait_recv()
            lev_copy(turn, 2 * off, 2 * off + 1, field, partner, n_chip - 1 + off).start()

    def finish_field(turn, field):
        lev_copy(turn, 0, 1, field, partner, n_chip - 1).wait_recv()
        for off in range(1, n_chip):
            lev_copy(turn, 2 * off, 2 * off + 1, field, partner, n_chip - 1 + off).wait_recv()

    def mixed(turn, field):
        joined = jnp.concatenate([g_ref[turn, slot, field] for slot in range(n_lev)], axis=-1)
        return jnp.dot(joined, b_ref[turn], precision=highest, preferred_element_type=jnp.float32)

    for field in range(3):
        g_ref[0, 0, field] = x_ref[field]
        start_field(0, field)

    row = lax.broadcasted_iota(jnp.int32, (ROWS, LANES), 0)
    lane = lax.broadcasted_iota(jnp.int32, (ROWS, LANES), 1)
    group = lane // modes

    spread_row = lax.broadcasted_iota(jnp.int32, (modes, LANES), 0)
    spread_lane = lax.broadcasted_iota(jnp.int32, (modes, LANES), 1)
    repeat = jnp.where(spread_lane % modes == spread_row, 1.0, 0.0).astype(jnp.float32)
    big_row = lax.broadcasted_iota(jnp.int32, (LANES, LANES), 0) // modes
    big_lane = lax.broadcasted_iota(jnp.int32, (LANES, LANES), 1) // modes
    diagonal = big_row == big_lane
    for turn, mat_ref in enumerate((tm_ref, fm_ref)):
        mine = mat_ref[pl.ds(pl.multiple_of(lev * modes, modes), modes), :]
        tt_ref[...] = lax.dot_general(mine, repeat, (((0,), (0,)), ((), ())), precision=highest,
                                      preferred_element_type=jnp.float32)
        for off in range(n_chip):
            owner_chip = lax.rem(chip - off + n_chip, n_chip)
            for other in range(2):
                owner = owner_chip * 2 + (core if other == 0 else 1 - core)
                block = tt_ref[pl.ds(pl.multiple_of(owner * modes, modes), modes), :]
                tiled = jnp.concatenate([block] * chunks, axis=0)
                slot = 2 * off + other
                b_ref[turn, slot * LANES:(slot + 1) * LANES, :] = jnp.where(diagonal, tiled, 0.0)

    spacing = 2.0 * math.pi / lon_all

    def by_row(values):
        result = jnp.zeros((ROWS, LANES), jnp.float32)
        for number, value in enumerate(values):
            result = jnp.where(row == number, jnp.float32(value), result)
        return result

    faces = [math.sin((j + 1.0) * spacing) for j in range(ROWS - 1)] + [0.0]
    centre = by_row([math.sin((j + 0.5) * spacing) for j in range(ROWS)])
    face = by_row(faces)
    below = by_row([0.0] + faces[:-1])
    inv_centre = 1.0 / centre
    k = jnp.broadcast_to(k_ref[...], (ROWS, LANES))
    weight_p = centre / k

    def power(base, exponent):
        result, square = None, base
        while exponent:
            if exponent & 1:
                result = square if result is None else result * square
            exponent >>= 1
            if exponent:
                square = square * square
        return jnp.ones_like(base) if result is None else result

    def lane_power(base, index):
        result, square, bit = jnp.ones_like(base), base, 1
        while bit < chunks:
            result = jnp.where((index & bit) != 0, result * square, result)
            square = square * square
            bit *= 2
        return result

    class Line:
        pass

    lines = []
    for t in range(SOLVES):
        line = Line()
        g = jnp.full((ROWS, LANES), sh_ref[t], jnp.float32)
        coef = k * inv_centre * inv_centre
        half = 0.5 * (g * g + k * (face + below) * inv_centre) / coef
        q = half + jnp.sqrt(half * (half + 2.0))
        line.r = 1.0 / (1.0 + q)
        gamma = line.r / (coef * (q * line.r) * (1.0 + line.r))
        line.inv_r = 1.0 + q
        line.inv_g = 1.0 / g
        line.src_p = gamma * g
        line.src_d = gamma * k * inv_centre
        line.up = gamma * k * face * inv_centre
        line.down = gamma * k * below * inv_centre
        line.r_n = power(line.r, cells)
        line.weight_a = lane_power(line.r_n, chunks - 1 - group)
        line.weight_b = lane_power(line.r_n, group)
        r_block = power(line.r_n, chunks)
        inv_den = 1.0 / (1.0 - power(r_block, n_lon))
        block_powers = [inv_den]
        for d in range(1, n_lon):
            block_powers.append(block_powers[-1] * r_block)
        for d in range(n_lon):
            wt_ref[t, d] = jnp.where(group == 0, block_powers[d],
                                     jnp.where(group == 1, block_powers[(n_lon - 2 - d) % n_lon], 1.0))
        ones = jnp.ones((1, ROWS, LANES), jnp.float32)
        wb_ref[t, 0:1] = ones
        wa_ref[t, cells - 1:cells] = ones
        step, factor = 1, line.r
        while step < cells:
            wb_ref[t, step:2 * step] = wb_ref[t, 0:step] * factor
            wa_ref[t, cells - 2 * step:cells - step] = wa_ref[t, cells - step:cells] * factor
            factor = factor * factor
            step *= 2
        lines.append(line)

    for field, target in enumerate((u_ref, v_ref, p_ref)):
        relay_field(0, field)
        finish_field(0, field)
        target[0, 0:cells] = mixed(0, field).reshape(cells, ROWS, LANES)

    def lane_total(tile):
        step = modes
        while step < LANES:
            tile = tile + pltpu.roll(tile, step, 1)
            step *= 2
        return tile

    def spread(tile, number):
        return lane_total(jnp.where(group == number, tile, 0.0))

    def dots_tile(values):
        tile = jnp.zeros((ROWS, LANES), jnp.float32)
        for number, value in enumerate(values):
            tile = jnp.where(row == number, jnp.sum(value, axis=0, keepdims=True), tile)
        return lane_total(tile)

    def product(first, second):
        total = (centre * (u_ref[first] * u_ref[second]) + face * (v_ref[first] * v_ref[second])
                 + weight_p * (p_ref[first, 0:cells] * p_ref[second, 0:cells]))
        return jnp.sum(total, axis=0)

    def send(x, tiles):
        count, base = TILES[x], n_lon * OFFSETS[x]
        for number, tile in enumerate(tiles):
            sbuf[OFFSETS[x] + number] = tile
            rbuf[base + (n_lon - 1) * count + number] = tile
        for off in range(1, n_lon):
            pltpu.make_async_remote_copy(
                src_ref=sbuf.at[pl.ds(OFFSETS[x], count)],
                dst_ref=rbuf.at[pl.ds(base + (off - 1) * count, count)],
                send_sem=lon_send.at[x],
                recv_sem=lon_recv.at[x],
                device_id=(lev, lax.rem(lon + off, n_lon)),
                device_id_type=MESH,
            ).start()

    def whole_copy(x):
        part = rbuf.at[pl.ds(n_lon * OFFSETS[x], (n_lon - 1) * TILES[x])]
        return pltpu.make_async_remote_copy(
            src_ref=part, dst_ref=part, send_sem=lon_send.at[x], recv_sem=lon_recv.at[x],
            device_id=(lev, lax.rem(lon + 1, n_lon)), device_id_type=MESH,
        )

    def received(x, number, t=None):
        count, base = TILES[x], n_lon * OFFSETS[x]
        terms = []
        for d in range(n_lon):
            tile = rbuf[base + d * count + number]
            terms.append(tile if t is None else tile * wt_ref[t, d])
        while len(terms) > 1:
            terms = [sum(terms[i:i + 2][1:], terms[i]) for i in range(0, len(terms), 2)]
        return terms[0]

    def ends(t, slot, carry):
        line = lines[t]
        source = src_ref[slot]
        end_a = jnp.sum(wa_ref[t] * source, axis=0) + carry * line.inv_r
        end_b = jnp.sum(wb_ref[t] * source, axis=0) + carry * line.r_n
        return end_a, end_b

    def ends_tile(t, pair, dots=None):
        line = lines[t]
        total_a = lane_total(pair[0] * line.weight_a)
        total_b = lane_total(pair[1] * line.weight_b)
        rest = jnp.zeros_like(total_a) if dots is None else dots
        return jnp.where(group == 0, total_a, jnp.where(group == 1, total_b, rest))

    def local_prefix(t, pair):
        line = lines[t]
        ahead = jnp.where(group >= 1, pltpu.roll(pair[0], modes, 1), 0.0)
        behind = jnp.where(group < chunks - 1, pltpu.roll(pair[1], LANES - modes, 1), 0.0)
        step, factor = 1, line.r_n
        while step < chunks:
            ahead = ahead + jnp.where(group >= step, factor * pltpu.roll(ahead, step * modes, 1), 0.0)
            behind = behind + jnp.where(group < chunks - step,
                                        factor * pltpu.roll(behind, LANES - step * modes, 1), 0.0)
            factor = factor * factor
            step *= 2
        return ahead, behind

    def runs(t, carries):
        r = lines[t].r
        zero = jnp.zeros((ROWS, LANES), jnp.float32)

        def step(i, state):
            j = cells - 1 - i
            following = []
            for slot, (a, b) in enumerate(state):
                a = r * a + src_ref[slot, i]
                fa_ref[slot, i] = a
                b = r * b
                fb_ref[slot, j] = b
                following.append((a, b + src_ref[slot, j]))
            return tuple(following)

        lax.fori_loop(0, cells, step, tuple((zero, carry) for carry in carries), unroll=8)

    def incoming(t, x, number, local, tile=None):
        line = lines[t]
        if tile is None:
            tile = received(x, number, t)
        in_a = spread(tile, 0) * line.weight_b + local[0]
        in_b = spread(tile, 1) * line.weight_a + local[1]
        return in_a, in_b

    def first_source(t, vector, slot):
        line = lines[t]
        flux = face * v_ref[vector]
        below_flux = pltpu.roll(flux, 1, 1)
        rest = line.src_p * p_ref[vector, 0:cells] - line.src_d * (u_ref[vector] + flux - below_flux)
        src_ref[slot] = rest
        src_ref[slot, 1:cells] = src_ref[slot, 1:cells] + line.src_d * u_ref[vector, 0:cells - 1]
        return line.src_d * u_ref[vector, cells - 1]

    def coupled(t):
        line = lines[t]
        solved = sol_ref[...]
        src_ref[0] = (src_ref[3] + line.up * pltpu.roll(solved, ROWS - 1, 1)
                      + line.down * pltpu.roll(solved, 1, 1))

    def scalar(tile, number):
        return jnp.broadcast_to(tile[number:number + 1, :], (ROWS, LANES))

    norms = []
    for t in range(SOLVES):
        line = lines[t]
        x = 3 * t
        vectors = [t] + list(range(t))
        carries, pairs = [], []
        for slot, vector in enumerate(vectors):
            carries.append(first_source(t, vector, slot))
            pairs.append(ends(t, slot, carries[-1]))
        dots = dots_tile([product(i, t) for i in range(t)]) if t else None
        if t == 0:
            dots = pltpu.roll(p_ref[0, 0], (3 * modes) % LANES, 1)
        send(x, [ends_tile(t, pair, dots if n == 0 else None) for n, pair in enumerate(pairs)])
        runs(t, carries)
        locals_ = [local_prefix(t, pair) for pair in pairs]
        whole_copy(x).wait_recv()
        tile = received(x, 0, t)
        carry, pair = carries[0], pairs[0]
        inc = incoming(t, x, 0, locals_[0], tile)
        ahead, behind, source = fa_ref[0], fb_ref[0], src_ref[0]
        coefs = []
        if t == 0:
            halo = spread(rbuf[n_lon * OFFSETS[x] + (n_lon - 2) * TILES[x]], 3)
            p_ref[0, cells] = jnp.where(group == chunks - 1, halo, pltpu.roll(p_ref[0, 0], LANES - modes, 1))
        else:
            sums = spread(tile, 2)
            for i in range(t):
                c = scalar(sums, i)
                coefs.append(c)
                other = incoming(t, x, i + 1, locals_[i + 1])
                inc = (inc[0] - c * other[0], inc[1] - c * other[1])
                carry = carry - c * carries[i + 1]
                ahead = ahead - c * fa_ref[i + 1]
                behind = behind - c * fb_ref[i + 1]
                source = source - c * src_ref[i + 1]
        src_ref[3] = source
        sol_ref[...] = (ahead + behind + wb_ref[t] * (line.r * inc[0]) + wa_ref[t] * (line.r * inc[1]))
        coupled(t)
        pair = ends(t, 0, carry)
        send(x + 1, [ends_tile(t, pair)])
        runs(t, [carry])
        local = local_prefix(t, pair)
        if t:
            for ref in (u_ref, v_ref, p_ref):
                value = ref[t]
                for i in range(t):
                    value = value - coefs[i] * ref[i]
                ref[t] = value
        norm_dots = dots_tile([product(t, t)])
        whole_copy(x + 1).wait_recv()
        inc = incoming(t, x + 1, 0, local)
        sol_ref[...] = (fa_ref[0] + fb_ref[0] + wb_ref[t] * (line.r * inc[0]) + wa_ref[t] * (line.r * inc[1]))
        coupled(t)
        pair = ends(t, 0, carry)
        send(x + 2, [ends_tile(t, pair, norm_dots)])
        runs(t, [carry])
        local = local_prefix(t, pair)
        whole_copy(x + 2).wait_recv()
        tile = received(x + 2, 0, t)
        inc = incoming(t, x + 2, 0, local, tile)
        norm = jnp.sqrt(scalar(spread(tile, 2), 0) + epsilon)
        norms.append(norm)
        scale = 1.0 / norm
        for ref in (u_ref, v_ref, p_ref):
            ref[t] = ref[t] * scale
        p_ref[t + 1, 0:cells] = (fa_ref[0] + fb_ref[0] + wb_ref[t] * (line.r * inc[0])
                                 + wa_ref[t] * (line.r * inc[1])) * scale
        p_ref[t + 1, cells] = (line.r * (pair[0] + line.r_n * inc[0]) + inc[1]) * scale
        solved = p_ref[t + 1, 0:cells]
        u_ref[t + 1] = (u_ref[t] - (p_ref[t + 1, 1:cells + 1] - solved) * inv_centre) * line.inv_g
        north = jnp.where(row < ROWS - 1, 1.0, 0.0)
        v_ref[t + 1] = (v_ref[t] - (pltpu.roll(solved, ROWS - 1, 1) - solved) * north) * line.inv_g

    def half_product(first, second):
        solved = p_ref[second, 0:cells]
        east = p_ref[second, 1:cells + 1] - solved
        north = pltpu.roll(solved, ROWS - 1, 1) - solved
        return jnp.sum(u_ref[first] * east + face * (v_ref[first] * north), axis=0)

    pairs6 = [(0, 1), (0, 2), (1, 2), (0, 3), (1, 3), (2, 3)]
    skew_sums = [half_product(b, a) - half_product(a, b) for a, b in pairs6]
    grams = [product(0, 1), product(0, 2), product(1, 2), product(0, 0), product(1, 1), product(2, 2)]
    projections = [product(i, 3) for i in range(3)] + [product(3, 3)]
    values = skew_sums + grams + projections
    send(LAST, [dots_tile(values[:8]), dots_tile(values[8:])])
    whole_copy(LAST).wait_recv()
    total = [received(LAST, 0), received(LAST, 1)]
    small = [scalar(total[n // 8], n % 8) for n in range(16)]
    k01, k02, k12, k03, k13, k23 = small[0:6]
    g01, g02, g12, g00, g11, g22 = small[6:12]
    c0, c1, c2, square = small[12:16]
    norm_sq = (square - 2.0 * (c0 * c0 + c1 * c1 + c2 * c2)
               + (c0 * c0 * g00 + c1 * c1 * g11 + c2 * c2 * g22)
               + 2.0 * (c0 * c1 * g01 + c0 * c2 * g02 + c1 * c2 * g12))
    inv_last = 1.0 / jnp.sqrt(jnp.maximum(norm_sq, 0.0) + epsilon)
    a03 = (k03 - (c1 * k01 + c2 * k02)) * inv_last
    a13 = (k13 - (c2 * k12 - c0 * k01)) * inv_last
    a23 = (k23 + (c0 * k02 + c1 * k12)) * inv_last
    zero = jnp.zeros_like(k01)
    matrix = [[zero, k01, k02, a03], [-k01, zero, k12, a13], [-k02, -k12, zero, a23], [-a03, -a13, -a23, zero]]
    scaled = [[value * (1.0 / 2.0**SQUARINGS) for value in line_] for line_ in matrix]

    def times(first, second):
        return [[(first[i][0] * second[0][j] + first[i][1] * second[1][j])
                 + (first[i][2] * second[2][j] + first[i][3] * second[3][j]) for j in range(KDIM)]
                for i in range(KDIM)]

    excess = [[value * (1.0 / TAYLOR) for value in line_] for line_ in scaled]
    for degree in range(TAYLOR - 1, 0, -1):
        grown = times(scaled, excess)
        excess = [[(scaled[i][j] + grown[i][j]) * (1.0 / degree) for j in range(KDIM)] for i in range(KDIM)]

    def square_step(_, flat):
        current = [list(flat[KDIM * i:KDIM * (i + 1)]) for i in range(KDIM)]
        squared = times(current, current)
        return tuple(2.0 * current[i][j] + squared[i][j] for i in range(KDIM) for j in range(KDIM))

    flat = lax.fori_loop(0, SQUARINGS, square_step, tuple(v for line_ in excess for v in line_))
    column = [flat[KDIM * i] + (1.0 if i == 0 else 0.0) for i in range(KDIM)]
    last = norms[0] * column[3] * inv_last
    mix = [norms[0] * column[i] - last * c for i, c in enumerate((c0, c1, c2))] + [last]

    for field, ref in enumerate((u_ref, v_ref, p_ref)):
        stepped = mix[0] * ref[0, 0:cells]
        for b in range(1, KDIM):
            stepped = stepped + mix[b] * ref[b, 0:cells]
        g_ref[1, 0, field] = stepped.reshape(cells * ROWS, LANES)
        start_field(1, field)
    for field in range(3):
        relay_field(1, field)
        finish_field(1, field)
        out_ref[field] = mixed(1, field)

    for turn in range(2):
        for field in range(3):
            for off in range(1, n_chip):
                lev_copy(turn, 0, 2 * off, field, chip_peer(off), off - 1).wait_send()
                lev_copy(turn, 2 * off, 2 * off + 1, field, partner, n_chip - 1 + off).wait_send()
            lev_copy(turn, 0, 1, field, partner, n_chip - 1).wait_send()
    for x in range(len(TILES)):
        whole_copy(x).wait_send()


def body(n_lev, n_lon, wave_state, to_modes, from_modes, courant, shifts):
    fields, modes, rows, span = wave_state.shape
    chunks = LANES // modes
    cells = span // chunks
    packed = wave_state.reshape(fields, modes, rows, chunks, cells)
    packed = packed.transpose(0, 4, 2, 3, 1).reshape(fields, cells * rows, LANES)
    speeds = jnp.tile(courant, chunks)[None, :]
    total = sum(TILES)
    block = (cells, ROWS, LANES)
    f32 = jnp.float32
    vmem = pl.BlockSpec(memory_space=pltpu.VMEM)
    result = pl.pallas_call(
        functools.partial(kernel, n_lev, n_lon, span * n_lon, modes, cells),
        out_shape=jax.ShapeDtypeStruct(packed.shape, f32),
        in_specs=[vmem, vmem, vmem, vmem, pl.BlockSpec(memory_space=pltpu.SMEM)],
        out_specs=vmem,
        scratch_shapes=[
            pltpu.VMEM((2, n_lev, fields, cells * rows, LANES), f32),
            pltpu.VMEM((2, n_lev * LANES, LANES), f32),
            pltpu.VMEM((KDIM,) + block, f32),
            pltpu.VMEM((KDIM,) + block, f32),
            pltpu.VMEM((KDIM, cells + 1, ROWS, LANES), f32),
            pltpu.VMEM((4,) + block, f32),
            pltpu.VMEM((3,) + block, f32),
            pltpu.VMEM((3,) + block, f32),
            pltpu.VMEM(block, f32),
            pltpu.VMEM((SOLVES,) + block, f32),
            pltpu.VMEM((SOLVES,) + block, f32),
            pltpu.VMEM((SOLVES, n_lon, ROWS, LANES), f32),
            pltpu.VMEM((n_lev * modes, LANES), f32),
            pltpu.VMEM((total, ROWS, LANES), f32),
            pltpu.VMEM((n_lon * total, ROWS, LANES), f32),
            pltpu.SemaphoreType.DMA((2, n_lev - 1, 3)),
            pltpu.SemaphoreType.DMA((2, n_lev, 3)),
            pltpu.SemaphoreType.DMA((len(TILES),)),
            pltpu.SemaphoreType.DMA((len(TILES),)),
        ],
        compiler_params=pltpu.CompilerParams(
            collective_id=0, has_side_effects=True, vmem_limit_bytes=40 * 1024 * 1024),
        name="krylov",
    )(packed, to_modes, from_modes, speeds, shifts)
    result = result.reshape(fields, cells, rows, chunks, modes).transpose(0, 4, 2, 3, 1)
    return result.reshape(fields, modes, rows, span)


def solution(mesh):
    n_lev, n_lon = mesh.shape["lev"], mesh.shape["lon"]
    in_specs = (P(None, "lev", None, "lon"), P(), P(), P("lev"), P())
    out_specs = P(None, "lev", None, "lon")
    return jax.shard_map(functools.partial(body, n_lev, n_lon), mesh=mesh, in_specs=in_specs,
                         out_specs=out_specs, check_vma=False)
```

```python
import functools
import math

import jax
import jax.numpy as jnp
from jax import lax
from jax.experimental import pallas as pl
from jax.experimental.pallas import tpu as pltpu
from jax.sharding import PartitionSpec as P

KDIM = 4
SWEEPS = 3
SQUARINGS = 16
TAYLOR = 8
SOLVES = KDIM - 1
LANES = 128
ROWS = 8
MESH = pl.DeviceIdType.MESH
highest = lax.Precision.HIGHEST
epsilon = 1e-06

TILES = []
for _t in range(SOLVES):
    TILES += [1, 1, 1, _t + 1 if _t + 1 < SOLVES else 1]
TILES += [1]
OFFSETS = [sum(TILES[:x]) for x in range(len(TILES))]
LAST = len(TILES) - 1


def kernel(n_lev, n_lon, lon_all, modes, cells, halves, x_ref, tm_ref, fm_ref, k_ref, sh_ref, out_ref,
           g_ref, h_ref, coef_ref, b_ref, u_ref, v_ref, p_ref, src_ref, fa_ref, fb_ref, sol_ref, wa_ref, wb_ref,
           wt_ref, tt_ref, o_ref, sbuf, rbuf, lev_send, lev_recv, h_send, h_recv, coef_send, coef_recv, lon_send, lon_recv):
    chunks = LANES // modes
    n_chip = n_lev // 2
    lev = lax.axis_index("lev")
    lon = lax.axis_index("lon")
    chip, core = lev // 2, lev % 2
    partner = chip * 2 + (1 - core)

    def chip_peer(offset):
        return lax.rem(chip + offset, n_chip) * 2 + core

    barrier = pltpu.get_barrier_semaphore()
    for off in range(1, n_lon):
        pl.semaphore_signal(barrier, inc=1, device_id=(lev, lax.rem(lon + off, n_lon)), device_id_type=MESH)
    for off in range(1, n_lev):
        pl.semaphore_signal(barrier, inc=1, device_id=(lax.rem(lev + off, n_lev), lon), device_id_type=MESH)
    pl.semaphore_wait(barrier, n_lon + n_lev - 2)

    def lev_copy(turn, slot_from, slot_to, field, target, send_no):
        return pltpu.make_async_remote_copy(
            src_ref=g_ref.at[turn, slot_from, field],
            dst_ref=g_ref.at[turn, slot_to, field],
            send_sem=lev_send.at[turn, send_no, field],
            recv_sem=lev_recv.at[turn, slot_to, field],
            device_id=(target, lon),
            device_id_type=MESH,
        )

    def start_field(turn, field):
        for off in range(1, n_chip):
            lev_copy(turn, 0, 2 * off, field, chip_peer(off), off - 1).start()
        lev_copy(turn, 0, 1, field, partner, n_chip - 1).start()

    def relay_field(turn, field):
        for off in range(1, n_chip):
            lev_copy(turn, 2 * off, 2 * off, field, chip_peer(off), off - 1).wait_recv()
            lev_copy(turn, 2 * off, 2 * off + 1, field, partner, n_chip - 1 + off).start()

    def finish_field(turn, field):
        lev_copy(turn, 0, 1, field, partner, n_chip - 1).wait_recv()
        for off in range(1, n_chip):
            lev_copy(turn, 2 * off, 2 * off + 1, field, partner, n_chip - 1 + off).wait_recv()

    def sent_fields(turn):
        for field in range(3):
            for off in range(1, n_chip):
                lev_copy(turn, 0, 2 * off, field, chip_peer(off), off - 1).wait_send()
                lev_copy(turn, 2 * off, 2 * off + 1, field, partner, n_chip - 1 + off).wait_send()
            lev_copy(turn, 0, 1, field, partner, n_chip - 1).wait_send()

    def p_copy(t, slot_from, slot_to, target, send_no):
        return pltpu.make_async_remote_copy(
            src_ref=h_ref.at[t, slot_from],
            dst_ref=h_ref.at[t, slot_to],
            send_sem=h_send.at[t, send_no],
            recv_sem=h_recv.at[t, slot_to],
            device_id=(target, lon),
            device_id_type=MESH,
        )

    def start_p(t):
        for off in range(1, n_chip):
            p_copy(t, 0, 2 * off, chip_peer(off), off - 1).start()
        p_copy(t, 0, 1, partner, n_chip - 1).start()

    def relay_p(t):
        for off in range(1, n_chip):
            p_copy(t, 2 * off, 2 * off, chip_peer(off), off - 1).wait_recv()
            p_copy(t, 2 * off, 2 * off + 1, partner, n_chip - 1 + off).start()

    def finish_p(t):
        p_copy(t, 0, 1, partner, n_chip - 1).wait_recv()
        for off in range(1, n_chip):
            p_copy(t, 2 * off, 2 * off + 1, partner, n_chip - 1 + off).wait_recv()

    def coef_whole():
        part = coef_ref.at[pl.ds(1, n_lev - 1)]
        return pltpu.make_async_remote_copy(
            src_ref=part, dst_ref=part, send_sem=coef_send.at[0], recv_sem=coef_recv.at[0],
            device_id=(partner, lon), device_id_type=MESH,
        )

    def mixed(turn, blocks):
        joined = jnp.concatenate(blocks, axis=-1)
        return jnp.dot(joined, b_ref[turn], precision=highest, preferred_element_type=jnp.float32)

    row = lax.broadcasted_iota(jnp.int32, (ROWS, LANES), 0)
    lane = lax.broadcasted_iota(jnp.int32, (ROWS, LANES), 1)
    group = lane // modes
    together = LANES // cells
    tall_group = lax.broadcasted_iota(jnp.int32, (cells, LANES), 1) // modes % together

    def turned(tile, steps):
        steps = steps * modes % LANES
        return pltpu.roll(tile, steps, 1) if steps else tile

    def chosen(tiles):
        result = tiles[0]
        for number in range(1, together):
            result = jnp.where(tall_group == number, tiles[number], result)
        return result

    def pack(field):
        for first in range(0, ROWS, together):
            stack = jnp.concatenate(
                [x_ref[field, :, first + n, half * LANES:(half + 1) * LANES]
                 for half in range(halves) for n in range(together)], axis=0)
            flipped = stack.T
            parts = [flipped[c * cells:(c + 1) * cells] for c in range(together)]
            for n in range(together):
                g_ref[0, 0, field, pl.ds(first + n, cells, stride=ROWS), :] = chosen(
                    [turned(parts[c], c - n) for c in range(together)])

    def unpack(field):
        for first in range(0, ROWS, together):
            rows = [o_ref[pl.ds(first + n, cells, stride=ROWS), :] for n in range(together)]
            flipped = jnp.concatenate(
                [chosen([turned(rows[n], n - c) for n in range(together)]) for c in range(together)], axis=0)
            stack = flipped.T
            for half in range(halves):
                for n in range(together):
                    at = (half * together + n) * modes
                    out_ref[field, :, first + n, half * LANES:(half + 1) * LANES] = stack[at:at + modes]

    for field in range(3):
        pack(field)
        start_field(0, field)

    spread_row = lax.broadcasted_iota(jnp.int32, (modes, LANES), 0)
    spread_lane = lax.broadcasted_iota(jnp.int32, (modes, LANES), 1)
    repeat = jnp.where(spread_lane % modes == spread_row, 1.0, 0.0).astype(jnp.float32)
    big_row = lax.broadcasted_iota(jnp.int32, (LANES, LANES), 0) // modes
    big_lane = lax.broadcasted_iota(jnp.int32, (LANES, LANES), 1) // modes
    diagonal = big_row == big_lane
    for turn, mat_ref in enumerate((tm_ref, fm_ref)):
        mine = mat_ref[pl.ds(pl.multiple_of(lev * modes, modes), modes), :]
        tt_ref[...] = lax.dot_general(mine, repeat, (((0,), (0,)), ((), ())), precision=highest,
                                      preferred_element_type=jnp.float32)
        for off in range(n_chip):
            owner_chip = lax.rem(chip - off + n_chip, n_chip)
            for other in range(2):
                owner = owner_chip * 2 + (core if other == 0 else 1 - core)
                block = tt_ref[pl.ds(pl.multiple_of(owner * modes, modes), modes), :]
                tiled = jnp.concatenate([block] * chunks, axis=0)
                slot = 2 * off + other
                b_ref[turn, slot * LANES:(slot + 1) * LANES, :] = jnp.where(diagonal, tiled, 0.0)

    spacing = 2.0 * math.pi / lon_all

    def by_row(values):
        result = jnp.zeros((ROWS, LANES), jnp.float32)
        for number, value in enumerate(values):
            result = jnp.where(row == number, jnp.float32(value), result)
        return result

    faces = [math.sin((j + 1.0) * spacing) for j in range(ROWS - 1)] + [0.0]
    centre = by_row([math.sin((j + 0.5) * spacing) for j in range(ROWS)])
    face = by_row(faces)
    below = by_row([0.0] + faces[:-1])
    inv_centre = 1.0 / centre
    k = jnp.broadcast_to(k_ref[...], (ROWS, LANES))
    weight_p = centre / k

    def power(base, exponent):
        result, square = None, base
        while exponent:
            if exponent & 1:
                result = square if result is None else result * square
            exponent >>= 1
            if exponent:
                square = square * square
        return jnp.ones_like(base) if result is None else result

    def lane_power(base, index):
        result, square, bit = jnp.ones_like(base), base, 1
        while bit < chunks:
            result = jnp.where((index & bit) != 0, result * square, result)
            square = square * square
            bit *= 2
        return result

    class Line:
        pass

    lines = []
    for t in range(SOLVES):
        line = Line()
        g = jnp.full((ROWS, LANES), sh_ref[t], jnp.float32)
        coef = k * inv_centre * inv_centre
        half = 0.5 * (g * g + k * (face + below) * inv_centre) / coef
        q = half + jnp.sqrt(half * (half + 2.0))
        line.r = 1.0 / (1.0 + q)
        gamma = line.r / (coef * (q * line.r) * (1.0 + line.r))
        line.inv_r = 1.0 + q
        line.inv_g = 1.0 / g
        line.src_p = gamma * g
        line.src_d = gamma * k * inv_centre
        line.up = gamma * k * face * inv_centre
        line.down = gamma * k * below * inv_centre
        line.r_n = power(line.r, cells)
        line.weight_a = lane_power(line.r_n, chunks - 1 - group)
        line.weight_b = lane_power(line.r_n, group)
        r_block = power(line.r_n, chunks)
        inv_den = 1.0 / (1.0 - power(r_block, n_lon))
        block_powers = [inv_den]
        for d in range(1, n_lon):
            block_powers.append(block_powers[-1] * r_block)
        for d in range(n_lon):
            wt_ref[t, d] = jnp.where(group == 0, block_powers[d],
                                     jnp.where(group == 1, block_powers[(n_lon - 2 - d) % n_lon], 1.0))
        ones = jnp.ones((1, ROWS, LANES), jnp.float32)
        wb_ref[t, 0:1] = ones
        wa_ref[t, cells - 1:cells] = ones
        step, factor = 1, line.r
        while step < cells:
            wb_ref[t, step:2 * step] = wb_ref[t, 0:step] * factor
            wa_ref[t, cells - 2 * step:cells - step] = wa_ref[t, cells - step:cells] * factor
            factor = factor * factor
            step *= 2
        lines.append(line)

    for field, target in enumerate((u_ref, v_ref, p_ref)):
        relay_field(0, field)
        finish_field(0, field)
        modal = mixed(0, [g_ref[0, slot, field] for slot in range(n_lev)])
        target[0, 0:cells] = modal.reshape(cells, ROWS, LANES)
        g_ref[1, 0, field] = modal
        start_field(1, field)

    def lane_total(tile):
        step = modes
        while step < LANES:
            tile = tile + pltpu.roll(tile, step, 1)
            step *= 2
        return tile

    def spread(tile, number):
        return lane_total(jnp.where(group == number, tile, 0.0))

    def dots_tile(values):
        tile = jnp.zeros((ROWS, LANES), jnp.float32)
        for number, value in enumerate(values):
            tile = jnp.where(row == number, jnp.sum(value, axis=0, keepdims=True), tile)
        return lane_total(tile)

    def product(first, second):
        total = (centre * (u_ref[first] * u_ref[second]) + face * (v_ref[first] * v_ref[second])
                 + weight_p * (p_ref[first, 0:cells] * p_ref[second, 0:cells]))
        return jnp.sum(total, axis=0)

    def send(x, tiles):
        count, base = TILES[x], n_lon * OFFSETS[x]
        for number, tile in enumerate(tiles):
            sbuf[OFFSETS[x] + number] = tile
            rbuf[base + (n_lon - 1) * count + number] = tile
        for off in range(1, n_lon):
            pltpu.make_async_remote_copy(
                src_ref=sbuf.at[pl.ds(OFFSETS[x], count)],
                dst_ref=rbuf.at[pl.ds(base + (off - 1) * count, count)],
                send_sem=lon_send.at[x],
                recv_sem=lon_recv.at[x],
                device_id=(lev, lax.rem(lon + off, n_lon)),
                device_id_type=MESH,
            ).start()

    def whole_copy(x):
        part = rbuf.at[pl.ds(n_lon * OFFSETS[x], (n_lon - 1) * TILES[x])]
        return pltpu.make_async_remote_copy(
            src_ref=part, dst_ref=part, send_sem=lon_send.at[x], recv_sem=lon_recv.at[x],
            device_id=(lev, lax.rem(lon + 1, n_lon)), device_id_type=MESH,
        )

    def received(x, number, t=None):
        count, base = TILES[x], n_lon * OFFSETS[x]
        terms = []
        for d in range(n_lon):
            tile = rbuf[base + d * count + number]
            terms.append(tile if t is None else tile * wt_ref[t, d])
        while len(terms) > 1:
            terms = [sum(terms[i:i + 2][1:], terms[i]) for i in range(0, len(terms), 2)]
        return terms[0]

    def ends(t, slot, carry):
        line = lines[t]
        source = src_ref[slot]
        end_a = jnp.sum(wa_ref[t] * source, axis=0) + carry * line.inv_r
        end_b = jnp.sum(wb_ref[t] * source, axis=0) + carry * line.r_n
        return end_a, end_b

    def ends_tile(t, pair, dots=None):
        line = lines[t]
        total_a = lane_total(pair[0] * line.weight_a)
        total_b = lane_total(pair[1] * line.weight_b)
        rest = jnp.zeros_like(total_a) if dots is None else dots
        return jnp.where(group == 0, total_a, jnp.where(group == 1, total_b, rest))

    def local_prefix(t, pair):
        line = lines[t]
        ahead = jnp.where(group >= 1, pltpu.roll(pair[0], modes, 1), 0.0)
        behind = jnp.where(group < chunks - 1, pltpu.roll(pair[1], LANES - modes, 1), 0.0)
        step, factor = 1, line.r_n
        while step < chunks:
            ahead = ahead + jnp.where(group >= step, factor * pltpu.roll(ahead, step * modes, 1), 0.0)
            behind = behind + jnp.where(group < chunks - step,
                                        factor * pltpu.roll(behind, LANES - step * modes, 1), 0.0)
            factor = factor * factor
            step *= 2
        return ahead, behind

    def runs(t, carries, slots):
        r = lines[t].r
        zero = jnp.zeros((ROWS, LANES), jnp.float32)

        def step(i, state):
            j = cells - 1 - i
            following = []
            for slot, (a, b) in zip(slots, state):
                a = r * a + src_ref[slot, i]
                fa_ref[slot, i] = a
                b = r * b
                fb_ref[slot, j] = b
                following.append((a, b + src_ref[slot, j]))
            return tuple(following)

        lax.fori_loop(0, cells, step, tuple((zero, carry) for carry in carries), unroll=8)

    def incoming(t, x, number, local, tile=None):
        line = lines[t]
        if tile is None:
            tile = received(x, number, t)
        in_a = spread(tile, 0) * line.weight_b + local[0]
        in_b = spread(tile, 1) * line.weight_a + local[1]
        return in_a, in_b

    def first_source(t, vector, slot):
        line = lines[t]
        flux = face * v_ref[vector]
        below_flux = pltpu.roll(flux, 1, 1)
        rest = line.src_p * p_ref[vector, 0:cells] - line.src_d * (u_ref[vector] + flux - below_flux)
        src_ref[slot] = rest
        src_ref[slot, 1:cells] = src_ref[slot, 1:cells] + line.src_d * u_ref[vector, 0:cells - 1]
        return line.src_d * u_ref[vector, cells - 1]

    def coupled(t):
        line = lines[t]
        solved = sol_ref[...]
        src_ref[0] = (src_ref[3] + line.up * pltpu.roll(solved, ROWS - 1, 1)
                      + line.down * pltpu.roll(solved, 1, 1))

    def scalar(tile, number):
        return jnp.broadcast_to(tile[number:number + 1, :], (ROWS, LANES))

    def half_product(first, second):
        solved = p_ref[second, 0:cells]
        east = p_ref[second, 1:cells + 1] - solved
        north = pltpu.roll(solved, ROWS - 1, 1) - solved
        return jnp.sum(u_ref[first] * east + face * (v_ref[first] * north), axis=0)

    def skew_sum(a, b):
        return half_product(b, a) - half_product(a, b)

    norms = []
    earlier = []
    scale = None
    none = jnp.zeros((ROWS, LANES), jnp.float32)
    wind_rows, height_rows = [], []
    wind = height = [none + 1.0, none, none, none]
    for t in range(SOLVES):
        line = lines[t]
        x = 4 * t
        carry = first_source(t, t, 0)
        pair = ends(t, 0, carry)
        if t:
            dots = dots_tile([product(i, t) for i in range(t)])
        else:
            dots = pltpu.roll(p_ref[0, 0], (3 * modes) % LANES, 1)
        send(x, [ends_tile(t, pair, dots)])
        runs(t, [carry], [0])
        local = local_prefix(t, pair)
        if t:
            whole_copy(x - 1).wait_recv()
            others = [incoming(t, x - 1, i, earlier[i][1]) for i in range(t)]
        whole_copy(x).wait_recv()
        tile = received(x, 0, t)
        inc = incoming(t, x, 0, local, tile)
        ahead, behind, source = fa_ref[0], fb_ref[0], src_ref[0]
        coefs = []
        if t == 0:
            halo = spread(rbuf[n_lon * OFFSETS[x] + (n_lon - 2) * TILES[x]], 3)
            p_ref[0, cells] = jnp.where(group == chunks - 1, halo, pltpu.roll(p_ref[0, 0], LANES - modes, 1))
        else:
            sums = spread(tile, 2)
            for i in range(t):
                c = scalar(sums, i)
                coefs.append(c)
                d = c * scale if i == t - 1 else c
                inc = (inc[0] - d * others[i][0], inc[1] - d * others[i][1])
                carry = carry - d * earlier[i][0]
                ahead = ahead - d * fa_ref[i + 1]
                behind = behind - d * fb_ref[i + 1]
                source = source - d * src_ref[i + 1]
        src_ref[3] = source
        sol_ref[...] = (ahead + behind + wb_ref[t] * (line.r * inc[0]) + wa_ref[t] * (line.r * inc[1]))
        coupled(t)
        pair = ends(t, 0, carry)
        send(x + 1, [ends_tile(t, pair)])
        runs(t, [carry], [0])
        local = local_prefix(t, pair)
        if t:
            for ref in (u_ref, v_ref, p_ref):
                value = ref[t]
                for i in range(t):
                    value = value - coefs[i] * ref[i]
                ref[t] = value
        norm_dots = dots_tile([product(t, t)])
        if t == 1:
            for field in range(3):
                relay_field(1, field)
        whole_copy(x + 1).wait_recv()
        inc = incoming(t, x + 1, 0, local)
        sol_ref[...] = (fa_ref[0] + fb_ref[0] + wb_ref[t] * (line.r * inc[0]) + wa_ref[t] * (line.r * inc[1]))
        coupled(t)
        pair = ends(t, 0, carry)
        send(x + 2, [ends_tile(t, pair, norm_dots)])
        runs(t, [carry], [0])
        local = local_prefix(t, pair)
        if t + 1 < SOLVES:
            carries = [first_source(t + 1, i, i + 1) for i in range(t + 1)]
            pairs = [ends(t + 1, i + 1, carries[i]) for i in range(t + 1)]
            send(x + 3, [ends_tile(t + 1, other) for other in pairs])
            runs(t + 1, carries, [i + 1 for i in range(t + 1)])
            earlier = [(carries[i], local_prefix(t + 1, pairs[i])) for i in range(t + 1)]
        else:
            send(x + 3, [dots_tile([skew_sum(0, 1), skew_sum(0, 2), skew_sum(1, 2), product(0, 1),
                                    product(0, 2), product(1, 2), product(1, 1), product(2, 2)])])
        if t:
            relay_p(t - 1)
        whole_copy(x + 2).wait_recv()
        tile = received(x + 2, 0, t)
        inc = incoming(t, x + 2, 0, local, tile)
        norm = jnp.sqrt(scalar(spread(tile, 2), 0) + epsilon)
        norms.append(norm)
        scale = 1.0 / norm
        for i in range(t):
            wind = [w - coefs[i] * e for w, e in zip(wind, wind_rows[i])]
            height = [w - coefs[i] * e for w, e in zip(height, height_rows[i])]
        wind_rows.append([w * scale for w in wind])
        height_rows.append([w * scale for w in height])
        wind = [(w + (1.0 if n == t + 1 else 0.0)) * line.inv_g for n, w in enumerate(wind_rows[t])]
        height = [none + (1.0 if n == t + 1 else 0.0) for n in range(KDIM)]
        for ref in (u_ref, v_ref, p_ref):
            ref[t] = ref[t] * scale
        p_ref[t + 1, 0:cells] = (fa_ref[0] + fb_ref[0] + wb_ref[t] * (line.r * inc[0])
                                 + wa_ref[t] * (line.r * inc[1])) * scale
        p_ref[t + 1, cells] = (line.r * (pair[0] + line.r_n * inc[0]) + inc[1]) * scale
        h_ref[t, 0] = p_ref[t + 1].reshape((cells + 1) * ROWS, LANES)
        start_p(t)
        solved = p_ref[t + 1, 0:cells]
        u_ref[t + 1] = (u_ref[t] - (p_ref[t + 1, 1:cells + 1] - solved) * inv_centre) * line.inv_g
        north = jnp.where(row < ROWS - 1, 1.0, 0.0)
        v_ref[t + 1] = (v_ref[t] - (pltpu.roll(solved, ROWS - 1, 1) - solved) * north) * line.inv_g

    values = [skew_sum(i, 3) for i in range(3)] + [product(i, 3) for i in range(3)]
    values += [product(3, 3), product(0, 0)]
    send(LAST, [dots_tile(values)])
    whole_copy(LAST - 1).wait_recv()
    total = received(LAST - 1, 0)
    k01, k02, k12, g01, g02, g12, g11, g22 = [scalar(total, n) for n in range(ROWS)]
    k02, k12, g02, g12, g22 = k02 * scale, k12 * scale, g02 * scale, g12 * scale, g22 * scale * scale
    whole_copy(LAST).wait_recv()
    total = received(LAST, 0)
    k03, k13, k23, c0, c1, c2, square, g00 = [scalar(total, n) for n in range(ROWS)]
    norm_sq = (square - 2.0 * (c0 * c0 + c1 * c1 + c2 * c2)
               + (c0 * c0 * g00 + c1 * c1 * g11 + c2 * c2 * g22)
               + 2.0 * (c0 * c1 * g01 + c0 * c2 * g02 + c1 * c2 * g12))
    inv_last = 1.0 / jnp.sqrt(jnp.maximum(norm_sq, 0.0) + epsilon)
    a03 = (k03 - (c1 * k01 + c2 * k02)) * inv_last
    a13 = (k13 - (c2 * k12 - c0 * k01)) * inv_last
    a23 = (k23 + (c0 * k02 + c1 * k12)) * inv_last
    zero = jnp.zeros_like(k01)
    matrix = [[zero, k01, k02, a03], [-k01, zero, k12, a13], [-k02, -k12, zero, a23], [-a03, -a13, -a23, zero]]
    scaled = [[value * (1.0 / 2.0**SQUARINGS) for value in line_] for line_ in matrix]

    def times(first, second):
        return [[(first[i][0] * second[0][j] + first[i][1] * second[1][j])
                 + (first[i][2] * second[2][j] + first[i][3] * second[3][j]) for j in range(KDIM)]
                for i in range(KDIM)]

    excess = [[value * (1.0 / TAYLOR) for value in line_] for line_ in scaled]
    for degree in range(TAYLOR - 1, 0, -1):
        grown = times(scaled, excess)
        excess = [[(scaled[i][j] + grown[i][j]) * (1.0 / degree) for j in range(KDIM)] for i in range(KDIM)]

    def square_step(_, flat):
        current = [list(flat[KDIM * i:KDIM * (i + 1)]) for i in range(KDIM)]
        squared = times(current, current)
        return tuple(2.0 * current[i][j] + squared[i][j] for i in range(KDIM) for j in range(KDIM))

    flat = lax.fori_loop(0, SQUARINGS, square_step, tuple(v for line_ in excess for v in line_))
    column = [flat[KDIM * i] + (1.0 if i == 0 else 0.0) for i in range(KDIM)]
    last = norms[0] * column[3] * inv_last
    mix = [norms[0] * column[i] - last * c for i, c in enumerate((c0, c1, c2))] + [last]
    wind_rows.append(wind)
    height_rows.append(height)
    coefs = none
    for n in range(KDIM):
        wind_sum = sum([mix[b] * wind_rows[b][n] for b in range(1, KDIM)], mix[0] * wind_rows[0][n])
        height_sum = sum([mix[b] * height_rows[b][n] for b in range(1, KDIM)], mix[0] * height_rows[0][n])
        coefs = jnp.where(row == n, wind_sum, jnp.where(row == KDIM + n, height_sum, coefs))

    coef_ref[0] = coefs
    for off in range(n_chip):
        for other in range(2):
            if off or other:
                target = lax.rem(chip + off, n_chip) * 2 + (core if other == 0 else 1 - core)
                pltpu.make_async_remote_copy(
                    src_ref=coef_ref.at[0], dst_ref=coef_ref.at[2 * off + other],
                    send_sem=coef_send.at[0], recv_sem=coef_recv.at[0],
                    device_id=(target, lon), device_id_type=MESH,
                ).start()
    relay_p(SOLVES - 1)
    sent_fields(0)
    for field in range(3):
        finish_field(1, field)
    for t in range(SOLVES):
        finish_p(t)
    coef_whole().wait_recv()
    blocks = [[], [], []]
    north = jnp.where(row < ROWS - 1, 1.0, 0.0)
    for slot in range(n_lev):
        weights = coef_ref[slot]
        first = [g_ref[1, slot, field].reshape(cells, ROWS, LANES) for field in range(3)]
        heights = [h_ref[t, slot].reshape(cells + 1, ROWS, LANES) for t in range(SOLVES)]
        joint = sum([scalar(weights, t + 1) * heights[t] for t in range(1, SOLVES)], scalar(weights, 1) * heights[0])
        keep = scalar(weights, 0)
        here = joint[0:cells]
        stepped = [keep * first[0] - inv_centre * (joint[1:cells + 1] - here),
                   keep * first[1] - north * (pltpu.roll(here, ROWS - 1, 1) - here),
                   sum([scalar(weights, KDIM + t + 1) * heights[t][0:cells] for t in range(SOLVES)],
                       scalar(weights, KDIM) * first[2])]
        for field in range(3):
            g_ref[0, slot, field] = stepped[field].reshape(cells * ROWS, LANES)
    for field in range(3):
        o_ref[...] = mixed(1, [g_ref[0, slot, field] for slot in range(n_lev)])
        unpack(field)

    for t in range(SOLVES):
        for off in range(1, n_chip):
            p_copy(t, 0, 2 * off, chip_peer(off), off - 1).wait_send()
            p_copy(t, 2 * off, 2 * off + 1, partner, n_chip - 1 + off).wait_send()
        p_copy(t, 0, 1, partner, n_chip - 1).wait_send()
    coef_whole().wait_send()
    sent_fields(1)
    for x in range(len(TILES)):
        whole_copy(x).wait_send()


def body(n_lev, n_lon, wave_state, to_modes, from_modes, courant, shifts):
    fields, modes, rows, span = wave_state.shape
    chunks = LANES // modes
    cells = span // chunks
    speeds = jnp.tile(courant, chunks)[None, :]
    total = sum(TILES)
    block = (cells, ROWS, LANES)
    f32 = jnp.float32
    vmem = pl.BlockSpec(memory_space=pltpu.VMEM)
    return pl.pallas_call(
        functools.partial(kernel, n_lev, n_lon, span * n_lon, modes, cells, span // LANES),
        out_shape=jax.ShapeDtypeStruct(wave_state.shape, f32),
        in_specs=[vmem, vmem, vmem, vmem, pl.BlockSpec(memory_space=pltpu.SMEM)],
        out_specs=vmem,
        scratch_shapes=[
            pltpu.VMEM((2, n_lev, fields, cells * rows, LANES), f32),
            pltpu.VMEM((SOLVES, n_lev, (cells + 1) * rows, LANES), f32),
            pltpu.VMEM((n_lev, ROWS, LANES), f32),
            pltpu.VMEM((2, n_lev * LANES, LANES), f32),
            pltpu.VMEM((KDIM,) + block, f32),
            pltpu.VMEM((KDIM,) + block, f32),
            pltpu.VMEM((KDIM, cells + 1, ROWS, LANES), f32),
            pltpu.VMEM((4,) + block, f32),
            pltpu.VMEM((3,) + block, f32),
            pltpu.VMEM((3,) + block, f32),
            pltpu.VMEM(block, f32),
            pltpu.VMEM((SOLVES,) + block, f32),
            pltpu.VMEM((SOLVES,) + block, f32),
            pltpu.VMEM((SOLVES, n_lon, ROWS, LANES), f32),
            pltpu.VMEM((n_lev * modes, LANES), f32),
            pltpu.VMEM((cells * rows, LANES), f32),
            pltpu.VMEM((total, ROWS, LANES), f32),
            pltpu.VMEM((n_lon * total, ROWS, LANES), f32),
            pltpu.SemaphoreType.DMA((2, n_lev - 1, 3)),
            pltpu.SemaphoreType.DMA((2, n_lev, 3)),
            pltpu.SemaphoreType.DMA((SOLVES, n_lev - 1)),
            pltpu.SemaphoreType.DMA((SOLVES, n_lev)),
            pltpu.SemaphoreType.DMA((1,)),
            pltpu.SemaphoreType.DMA((1,)),
            pltpu.SemaphoreType.DMA((len(TILES),)),
            pltpu.SemaphoreType.DMA((len(TILES),)),
        ],
        compiler_params=pltpu.CompilerParams(
            collective_id=0, has_side_effects=True, vmem_limit_bytes=40 * 1024 * 1024),
        name="krylov",
    )(wave_state, to_modes, from_modes, speeds, shifts)


def solution(mesh):
    n_lev, n_lon = mesh.shape["lev"], mesh.shape["lon"]
    in_specs = (P(None, "lev", None, "lon"), P(), P(), P("lev"), P())
    out_specs = P(None, "lev", None, "lon")
    return jax.shard_map(functools.partial(body, n_lev, n_lon), mesh=mesh, in_specs=in_specs,
                         out_specs=out_specs, check_vma=False)
```
